256 devices in a mesh: seq: 64 (over z, y, core), head: 4 (over x).
Axes of the slice: x: 4, y: 4, z: 8, core: 2. Of those that a mesh axis runs over, the one named last changes fastest.
Arguments:
- queries: bfloat16 [64, 8192], P('seq', 'head')
- k_cache: bfloat16 [786432, 1024], P('seq', 'head')
- v_cache: bfloat16 [786432, 1024], P('seq', 'head'), may hold values from -6 to 6
- o_weight: bfloat16 [8192, 8192], P('head', 'seq'), may hold values from -0.0625 to 0.0625
- group_size: int32 [6], replicated, may hold values from 2 to 32, as said below
- group_start: int32 [6], replicated, may hold values from 0 to 62, as said below
- cache_len: int32 [6], replicated, may hold values from 1 to 393216, as said below
- owner: int32 [6], replicated, may hold values from 0 to 63, as said below
Outputs:
- projected: bfloat16 [6, 8192], P(None, 'seq')
The draws below stay inside these ranges and needn't reach their ends.
Inputs may be any that keep to these rules, and one draw needn't show every extreme that they name: `group_size`: each subgroup size is a power of two; one request has 32; the subgroup that ends at seq index 63 has 2. `group_start`: each start is a multiple of its group_size; the subgroups are disjoint and together cover all 64 seq indices. cache_len[r] is at most group_size[r] * 12288, and a request with 32 seq indices has exactly that. owner[r] lies inside request r's subgroup.
All inputs are finite; a program needn't handle non-finite values.
Results may differ from the reference program's by a relative error of at most 0.014.
Values may be sent and summed in bfloat16 or wider, within the bound.
A program may use at most 64 MiB of HBM per device.

```python
import jax
import jax.numpy as jnp
from jax import lax

MODEL_DIM = 8192
Q_HEADS = 64
KV_HEADS = 8
HEAD_DIM = 128
SLOT_DEV = 12288
REQ = 6
SLOTS = 786432
N_SEQ = 64


def subgroups(key):
    key = jax.random.fold_in(key, 700)
    index = jnp.arange(REQ, dtype=jnp.int32)
    half = N_SEQ // 2
    sizes = jnp.zeros((REQ,), jnp.int32).at[0].set(half).at[1].set(half)
    starts = jnp.zeros((REQ,), jnp.int32).at[1].set(half)
    for turn in range(2, REQ):
        ranking = jax.random.permutation(jax.random.fold_in(key, turn), REQ).astype(jnp.int32)
        splittable = (index >= 1) & (index < turn) & (sizes >= 4)
        at_end = (index < turn) & (starts + sizes == N_SEQ)
        end_one = jnp.argmax(at_end.astype(jnp.int32))
        end_size = jnp.sum(jnp.where(at_end, sizes, 0))
        needed = sum([(end_size > 2 << bit).astype(jnp.int32) for bit in range(8)])
        random_one = jnp.argmax(jnp.where(splittable, ranking, -1))
        chosen = jnp.where(REQ - turn <= needed, end_one, random_one)
        piece = sizes[chosen] // 2
        sizes = sizes.at[chosen].set(piece).at[turn].set(piece)
        starts = starts.at[turn].set(starts[chosen] + piece)
    order = jax.random.permutation(jax.random.fold_in(key, 99), REQ)
    return (sizes[order], starts[order])


def draw_group_size(key, part):
    sizes, starts = subgroups(key)
    return sizes


def draw_group_start(key, part):
    sizes, starts = subgroups(key)
    return starts


def draw_cache_len(key, part):
    sizes, starts = subgroups(key)
    key = jax.random.fold_in(key, 21)
    first = jax.random.fold_in(key, 0)
    capacity = sizes * SLOT_DEV
    lengths = jax.random.randint(first, (REQ,), capacity // 4 + 1, capacity + 1)
    full = jnp.argmax((sizes == N_SEQ // 2).astype(jnp.int32))
    return jnp.where(jnp.arange(REQ, dtype=jnp.int32) == full, capacity, lengths).astype(jnp.int32)


def draw_owner(key, part):
    sizes, starts = subgroups(key)
    key = jax.random.fold_in(key, 31)
    return (starts + jax.random.randint(key, (REQ,), 0, sizes)).astype(jnp.int32)


def draw_queries(key, part):
    key = jax.random.fold_in(key, 3)
    first = jax.random.fold_in(key, 0)
    noise = jax.random.normal(first, (N_SEQ, Q_HEADS, HEAD_DIM), jnp.float32)
    values = 3.0 * jnp.clip(noise, -6.0, 6.0)
    return values.reshape(N_SEQ, Q_HEADS * HEAD_DIM).astype(jnp.bfloat16)


def draw_k_cache(key, part):
    key = jax.random.fold_in(key, 5)
    first = jax.random.fold_in(key, 0)
    noise = jax.random.normal(first, (SLOTS, KV_HEADS, HEAD_DIM), jnp.float32)
    values = jnp.clip(noise, -6.0, 6.0)
    return values.reshape(SLOTS, KV_HEADS * HEAD_DIM).astype(jnp.bfloat16)


def level_of(own_key, extent, cuts, least, high):
    level = 1.0
    for dim, shards_of in cuts:
        steps = jax.random.uniform(jax.random.fold_in(jax.random.fold_in(own_key, 6), dim), (shards_of,), jnp.float32, least / len(cuts), high / len(cuts))
        level = level * jnp.repeat(jnp.exp(steps), extent[dim] // shards_of).reshape((-1,) + (1,) * (len(extent) - 1 - dim))
    return level


def normal_values(own_key, shape, spread, limit, cuts=(), kind=jnp.bfloat16):
    values = jax.random.normal(own_key, shape, jnp.float32) * spread
    if len(cuts) > 0:
        values = level_of(own_key, shape, cuts, -0.22, 0.18) * values
    return jnp.clip(values, min=-limit, max=limit).astype(kind)


def setup_inputs(seed: int = 0) -> dict:
    splits = jax.random.split(jax.random.key(seed), 9)
    return {
        "queries": draw_queries(jax.random.fold_in(splits[8], 71), 0),
        "k_cache": draw_k_cache(jax.random.fold_in(splits[8], 71), 0),
        "v_cache": normal_values(splits[2], (SLOTS, KV_HEADS * HEAD_DIM), 1.0, 6.0, ((0, 64), (1, 4))),
        "o_weight": normal_values(splits[3], (Q_HEADS * HEAD_DIM, MODEL_DIM), (Q_HEADS * HEAD_DIM) ** -0.5, 0.0625, ((0, 4), (1, 64))),
        "group_size": draw_group_size(jax.random.fold_in(splits[8], 71), 0),
        "group_start": draw_group_start(jax.random.fold_in(splits[8], 71), 0),
        "cache_len": draw_cache_len(jax.random.fold_in(splits[8], 71), 0),
        "owner": draw_owner(jax.random.fold_in(splits[8], 71), 0),
    }


NEG = -1e30


def reference(queries, k_cache, v_cache, o_weight, group_size, group_start, cache_len, owner):
    devices = jnp.arange(N_SEQ, dtype=jnp.int32)
    member = (devices[None, :] >= group_start[:, None]) & (devices[None, :] < (group_start + group_size)[:, None])
    request_of = jnp.sum(jnp.arange(REQ, dtype=jnp.int32)[:, None] * member.astype(jnp.int32), axis=0).astype(jnp.int32)
    groups = Q_HEADS // KV_HEADS
    asked = queries[owner].reshape(REQ, KV_HEADS, groups, HEAD_DIM).astype(jnp.float32)
    scale = HEAD_DIM ** -0.5

    def scores_of(device):
        request = request_of[device]
        keys = lax.dynamic_slice_in_dim(k_cache, (device * SLOT_DEV).astype(jnp.int32), SLOT_DEV, 0)
        keys = keys.reshape(SLOT_DEV, KV_HEADS, HEAD_DIM).astype(jnp.float32)
        scores = jnp.einsum("agd,sad->ags", asked[request], keys, precision=lax.Precision.HIGHEST) * scale
        place = (device - group_start[request]) * SLOT_DEV + jnp.arange(SLOT_DEV, dtype=jnp.int32)
        valid = place < cache_len[request]
        return scores, valid, request

    def local_peak(device):
        scores, valid, request = scores_of(device)
        return jnp.max(jnp.where(valid, scores, NEG), axis=-1)

    peaks = lax.map(local_peak, devices)
    top = jnp.max(jnp.where(member[:, :, None, None], peaks[None], NEG), axis=1)

    def local_sums(device):
        scores, valid, request = scores_of(device)
        expo = jnp.where(valid, jnp.exp(scores - top[request][..., None]), 0.0)
        weights = expo.astype(jnp.bfloat16).astype(jnp.float32)
        values = lax.dynamic_slice_in_dim(v_cache, (device * SLOT_DEV).astype(jnp.int32), SLOT_DEV, 0)
        values = values.reshape(SLOT_DEV, KV_HEADS, HEAD_DIM).astype(jnp.float32)
        outputs = jnp.einsum("ags,sad->agd", weights, values, precision=lax.Precision.HIGHEST)
        return jnp.sum(expo, axis=-1), outputs

    totals, outputs = lax.map(local_sums, devices)
    mask = member.astype(jnp.float32)
    total = jnp.einsum("rn,nag->rag", mask, totals, precision=lax.Precision.HIGHEST)
    summed = jnp.einsum("rn,nagd->ragd", mask, outputs, precision=lax.Precision.HIGHEST)
    attended = (summed / total[..., None]).reshape(REQ, Q_HEADS * HEAD_DIM).astype(jnp.bfloat16)
    return jnp.dot(attended, o_weight, preferred_element_type=jnp.float32).astype(jnp.bfloat16)
```

```python
import functools

import jax
import jax.numpy as jnp
from jax import lax
from jax.experimental import pallas as pl
from jax.experimental.pallas import tpu as pltpu
from jax.sharding import PartitionSpec as P

HEAD_DIM = 128
MESH = pl.DeviceIdType.MESH
LOG2E = 1.4426950408889634
SCALE = HEAD_DIM ** (-0.5)
EXPO = SCALE * LOG2E
NEG = -1e30 / SCALE
BLOCK = 32
PARTS = 4
CHUNK = 1024


def attend(query, k_vmem, v_vmem, live, slots):
    zero = jnp.zeros((8, HEAD_DIM), jnp.bfloat16)
    wide = jnp.concatenate(
        [
            jnp.concatenate([query[:8], zero], axis=1),
            jnp.concatenate([zero, query[8:]], axis=1),
        ],
        axis=0,
    )
    lane = lax.broadcasted_iota(jnp.int32, (16, CHUNK), 1)
    per_part = slots // PARTS
    found = []
    for part in range(PARTS):
        scores = []
        for first in range(part * per_part, (part + 1) * per_part, CHUNK):
            keys = k_vmem[first : first + CHUNK, :]
            score = lax.dot_general(
                wide, keys, (((1,), (1,)), ((), ())), preferred_element_type=jnp.float32
            )
            scores.append(jnp.where(lane < live - first, score, NEG))
        peak = functools.reduce(jnp.maximum, scores)
        peak = jnp.max(peak, axis=1, keepdims=True)
        total = jnp.zeros((16, CHUNK), jnp.float32)
        summed = jnp.zeros((16, 2 * HEAD_DIM), jnp.float32)
        for step, score in enumerate(scores):
            first = part * per_part + step * CHUNK
            expo = jnp.exp2((score - peak) * EXPO)
            total = total + expo
            summed = summed + jnp.dot(
                expo.astype(jnp.bfloat16),
                v_vmem[first : first + CHUNK, :],
                preferred_element_type=jnp.float32,
            )
        found.append((peak, jnp.sum(total, axis=1, keepdims=True), summed))
    top = functools.reduce(jnp.maximum, [peak for peak, _, _ in found])
    total = jnp.zeros((16, 1), jnp.float32)
    summed = jnp.zeros((16, 2 * HEAD_DIM), jnp.float32)
    for peak, part_total, part_summed in found:
        shrink = jnp.exp2((peak - top) * EXPO)
        total = total + part_total * shrink
        summed = summed + part_summed * shrink
    return top, total, summed


def kernel(
    q_ref,
    k_hbm,
    v_hbm,
    w_hbm,
    size_ref,
    start_ref,
    length_ref,
    owner_ref,
    out_ref,
    k_vmem,
    v_vmem,
    w_vmem,
    q_all,
    swap_out,
    swap_in,
    gathered,
    product,
    terms,
    load_sem,
    send_sem,
    recv_sem,
):
    me = lax.axis_index("seq")
    x = lax.axis_index("head")
    slots = k_hbm.shape[0]
    requests = size_ref.shape[0]
    base = (me // BLOCK) * BLOCK
    off = me - base
    core = me % 2
    chip = me // 2
    other = me + 1 - 2 * core
    chips = lax.axis_size("seq") // 2
    heads = lax.axis_size("head")
    half = w_hbm.shape[0] // 2

    loads = []
    for part in range(PARTS):
        rows = pl.ds(part * (slots // PARTS), slots // PARTS)
        loads.append(
            pltpu.make_async_copy(k_hbm.at[rows], k_vmem.at[rows], load_sem.at[part])
        )
    for part in range(PARTS):
        rows = pl.ds(part * (slots // PARTS), slots // PARTS)
        loads.append(
            pltpu.make_async_copy(v_hbm.at[rows], v_vmem.at[rows], load_sem.at[PARTS + part])
        )
    mine = pl.ds(pl.multiple_of(core * half, half), half)
    theirs = pl.ds(pl.multiple_of((1 - core) * half, half), half)
    loads.append(pltpu.make_async_copy(w_hbm.at[mine], w_vmem.at[0], load_sem.at[2 * PARTS]))
    for load in loads:
        load.start()

    def in_block(step):
        return base + (off + step) % BLOCK

    def far_chip(step):
        return ((chip + step) % chips) * 2 + core

    barrier = pltpu.get_barrier_semaphore()

    @pl.loop(1, BLOCK)
    def _(step):
        pl.semaphore_signal(barrier, 1, device_id={"seq": in_block(step)}, device_id_type=MESH)

    other_half = ((me // BLOCK + 1) % 2) * BLOCK + core

    @pl.loop(0, BLOCK // 2)
    def _(step):
        pl.semaphore_signal(
            barrier, 1, device_id={"seq": other_half + 2 * step}, device_id_type=MESH
        )

    for step in range(1, heads):
        across = (x + step) % heads
        for seq in (me, other):
            pl.semaphore_signal(
                barrier, 1, device_id={"seq": seq, "head": across}, device_id_type=MESH
            )

    query = q_ref[...].astype(jnp.float32)
    rows = [query[:, h * HEAD_DIM : (h + 1) * HEAD_DIM] for h in range(16)]
    q_all[off] = jnp.concatenate(rows, axis=0).astype(jnp.bfloat16)
    pl.semaphore_wait(barrier, (BLOCK - 1) + BLOCK // 2 + 2 * (heads - 1))

    @pl.loop(1, BLOCK)
    def _(step):
        pltpu.make_async_remote_copy(
            src_ref=q_all.at[off],
            dst_ref=q_all.at[off],
            send_sem=send_sem.at[0],
            recv_sem=recv_sem.at[0],
            device_id={"seq": in_block(step)},
            device_id_type=MESH,
        ).start()

    weight_copy = pltpu.make_async_remote_copy(
        src_ref=w_hbm.at[theirs],
        dst_ref=w_vmem.at[1],
        send_sem=send_sem.at[1],
        recv_sem=recv_sem.at[1],
        device_id={"seq": other},
        device_id_type=MESH,
    )
    weight_copy.start()

    my_start = jnp.int32(0)
    my_length = jnp.int32(0)
    my_owner = jnp.int32(0)
    for r in range(requests):
        inside = (me >= start_ref[r]) & (me < start_ref[r] + size_ref[r])
        my_start = my_start + jnp.where(inside, start_ref[r], 0)
        my_length = my_length + jnp.where(inside, length_ref[r], 0)
        my_owner = my_owner + jnp.where(inside, owner_ref[r], 0)
    live = my_length - (me - my_start) * slots

    for load in loads:
        load.wait()
    queries_in = q_all.at[pl.ds(0, BLOCK - 1)]
    queries_copy = pltpu.make_async_remote_copy(
        src_ref=queries_in,
        dst_ref=queries_in,
        send_sem=send_sem.at[0],
        recv_sem=recv_sem.at[0],
        device_id={"seq": other},
        device_id_type=MESH,
    )
    queries_copy.wait_recv()
    top, total, summed = attend(q_all[lax.rem(my_owner, BLOCK)], k_vmem, v_vmem, live, slots)

    first = core == 0
    low = (
        summed[:8, :HEAD_DIM],
        jnp.broadcast_to(top[:8], (8, HEAD_DIM)),
        jnp.broadcast_to(total[:8], (8, HEAD_DIM)),
    )
    high = (
        summed[8:, HEAD_DIM:],
        jnp.broadcast_to(top[8:], (8, HEAD_DIM)),
        jnp.broadcast_to(total[8:], (8, HEAD_DIM)),
    )
    for i in range(3):
        swap_out[8 * i : 8 * i + 8, :] = jnp.where(first, high[i], low[i])
    swap = pltpu.make_async_remote_copy(
        src_ref=swap_out,
        dst_ref=swap_in,
        send_sem=send_sem.at[2],
        recv_sem=recv_sem.at[2],
        device_id={"seq": other},
        device_id_type=MESH,
    )
    swap.start()
    summed, top, total = (jnp.where(first, low[i], high[i]) for i in range(3))
    swap.wait_recv()
    their_top = swap_in[8:16, :]
    new_top = jnp.maximum(top, their_top)
    shrink = jnp.exp2((top - new_top) * EXPO)
    their_shrink = jnp.exp2((their_top - new_top) * EXPO)
    gathered[chip, 0:8, :] = summed * shrink + swap_in[0:8, :] * their_shrink
    total = total * shrink + swap_in[16:24, :] * their_shrink
    lane = lax.broadcasted_iota(jnp.int32, (8, HEAD_DIM), 1)
    row = lax.broadcasted_iota(jnp.int32, (8, HEAD_DIM), 0)
    facts = jnp.where(lane == row, new_top, 0.0) + jnp.where(lane == row + 8, total, 0.0)
    gathered[chip, 8:9, :] = jnp.sum(facts, axis=0, keepdims=True)

    @pl.loop(1, chips)
    def _(step):
        pltpu.make_async_remote_copy(
            src_ref=gathered.at[chip, pl.ds(0, 9)],
            dst_ref=gathered.at[chip, pl.ds(0, 9)],
            send_sem=send_sem.at[3],
            recv_sem=recv_sem.at[3],
            device_id={"seq": far_chip(step)},
            device_id_type=MESH,
        ).start()

    starts = jnp.zeros((8, chips), jnp.int32)
    ends = jnp.zeros((8, chips), jnp.int32)
    request = lax.broadcasted_iota(jnp.int32, (8, chips), 0)
    seq_of = 2 * lax.broadcasted_iota(jnp.int32, (8, chips), 1)
    for r in range(requests):
        starts = jnp.where(request == r, start_ref[r], starts)
        ends = jnp.where(request == r, start_ref[r] + size_ref[r], ends)
    member = ((seq_of >= starts) & (seq_of < ends)).astype(jnp.float32).astype(jnp.bfloat16)
    seq_down = 2 * lax.broadcasted_iota(jnp.int32, (chips, HEAD_DIM), 0)
    serves = [
        (seq_down >= start_ref[r]) & (seq_down < start_ref[r] + size_ref[r])
        for r in range(requests)
    ]

    gathered_in = gathered.at[pl.ds(0, chips - 1), pl.ds(0, 9)]
    gathered_copy = pltpu.make_async_remote_copy(
        src_ref=gathered_in,
        dst_ref=gathered_in,
        send_sem=send_sem.at[3],
        recv_sem=recv_sem.at[3],
        device_id={"seq": other},
        device_id_type=MESH,
    )
    gathered_copy.wait_recv()

    facts = gathered[:, 8, :]
    totals = pltpu.roll(facts, HEAD_DIM - 8, 1)
    tops = jnp.zeros((chips, HEAD_DIM), jnp.float32)
    for r in range(requests):
        top = jnp.max(jnp.where(serves[r], facts, NEG), axis=0, keepdims=True)
        tops = jnp.where(serves[r], top, tops)
    lane = lax.broadcasted_iota(jnp.int32, (chips, HEAD_DIM), 1)
    factor = jnp.exp2(jnp.where(lane < 8, (facts - tops) * EXPO, 0.0))
    scaled = factor * totals
    sums = jnp.ones((chips, HEAD_DIM), jnp.float32)
    for r in range(requests):
        total = jnp.sum(jnp.where(serves[r], scaled, 0.0), axis=0, keepdims=True)
        sums = jnp.where(serves[r], total, sums)
    factor = factor / sums
    pieces = [gathered[:, h, :] * factor[:, h : h + 1] for h in range(8)]
    weighted = jnp.concatenate(pieces, axis=1).astype(jnp.bfloat16)
    attended = jnp.dot(member, weighted, preferred_element_type=jnp.float32).astype(jnp.bfloat16)

    weight_copy.wait_recv()
    slot = 2 * x + core
    product[0] = jnp.dot(attended, w_vmem[1], preferred_element_type=jnp.float32)
    ours = jnp.dot(attended, w_vmem[0], preferred_element_type=jnp.float32)
    product[1] = ours
    terms[slot] = ours

    def final(which, seq, across):
        return pltpu.make_async_remote_copy(
            src_ref=product.at[which],
            dst_ref=terms.at[slot],
            send_sem=send_sem.at[4],
            recv_sem=recv_sem.at[4],
            device_id={"seq": seq, "head": across},
            device_id_type=MESH,
        )

    for step in (2, 1, 3):
        final(0, other, (x + step) % heads).start()
        final(1, me, (x + step) % heads).start()
    final(0, other, x).start()

    terms_in = terms.at[pl.ds(0, 2 * heads - 1)]
    terms_copy = pltpu.make_async_remote_copy(
        src_ref=terms_in,
        dst_ref=terms_in,
        send_sem=send_sem.at[4],
        recv_sem=recv_sem.at[4],
        device_id={"seq": other},
        device_id_type=MESH,
    )
    terms_copy.wait_recv()
    out = terms[0]
    for i in range(1, 2 * heads):
        out = out + terms[i]
    out_ref[...] = out[:requests].astype(jnp.bfloat16)
    queries_copy.wait_send()
    weight_copy.wait_send()
    swap.wait_send()
    gathered_copy.wait_send()
    terms_copy.wait_send()


def per_device(queries, k_cache, v_cache, o_weight, group_size, group_start, cache_len, owner):
    requests = group_size.shape[0]
    slots, width = k_cache.shape
    rows, columns = o_weight.shape
    chips = lax.axis_size("seq") // 2
    heads = lax.axis_size("head")
    hbm = pl.BlockSpec(memory_space=pl.ANY)
    vmem = pl.BlockSpec(memory_space=pltpu.VMEM)
    smem = pl.BlockSpec(memory_space=pltpu.SMEM)
    return pl.pallas_call(
        kernel,
        out_shape=jax.ShapeDtypeStruct((requests, columns), jnp.bfloat16),
        in_specs=[vmem, hbm, hbm, hbm, smem, smem, smem, smem],
        out_specs=vmem,
        scratch_shapes=[
            pltpu.VMEM((slots, width), jnp.bfloat16),
            pltpu.VMEM((slots, width), jnp.bfloat16),
            pltpu.VMEM((2, rows // 2, columns), jnp.bfloat16),
            pltpu.VMEM((BLOCK, 16, HEAD_DIM), jnp.bfloat16),
            pltpu.VMEM((24, HEAD_DIM), jnp.float32),
            pltpu.VMEM((24, HEAD_DIM), jnp.float32),
            pltpu.VMEM((chips, 16, HEAD_DIM), jnp.float32),
            pltpu.VMEM((2, 8, columns), jnp.float32),
            pltpu.VMEM((2 * heads, 8, columns), jnp.float32),
            pltpu.SemaphoreType.DMA((2 * PARTS + 1,)),
            pltpu.SemaphoreType.DMA((5,)),
            pltpu.SemaphoreType.DMA((5,)),
        ],
        compiler_params=pltpu.CompilerParams(
            collective_id=0, has_side_effects=True, vmem_limit_bytes=56 * 1024 * 1024
        ),
    )(queries, k_cache, v_cache, o_weight, group_size, group_start, cache_len, owner)


def solution(mesh):
    in_specs = (
        P("seq", "head"),
        P("seq", "head"),
        P("seq", "head"),
        P("head", "seq"),
        P(),
        P(),
        P(),
        P(),
    )
    out_specs = P(None, "seq")
    return jax.shard_map(
        per_device, mesh=mesh, in_specs=in_specs, out_specs=out_specs, check_vma=False
    )
```

```python
import functools

import jax
import jax.numpy as jnp
from jax import lax
from jax.experimental import pallas as pl
from jax.experimental.pallas import tpu as pltpu
from jax.sharding import PartitionSpec as P

HEAD_DIM = 128
MESH = pl.DeviceIdType.MESH
LOG2E = 1.4426950408889634
SCALE = HEAD_DIM ** (-0.5)
EXPO = SCALE * LOG2E
NEG = -1e30 / SCALE
BLOCK = 32
WIDTH = 4
PARTS = 4
CHUNK = 1024
TURN = 256


def attend(query, k_turned, v_vmem, live, slots):
    lane = lax.broadcasted_iota(jnp.int32, (8, CHUNK), 1)
    per_part = slots // PARTS

    def score_part(part):
        scores = []
        for first in range(part * per_part, (part + 1) * per_part, CHUNK):
            keys = k_turned[:, first : first + CHUNK]
            score = jnp.dot(query, keys, preferred_element_type=jnp.float32)
            scores.append(jnp.where(lane < live - first, score, NEG))
        return scores

    def value_part(part, scores):
        peak = functools.reduce(jnp.maximum, scores)
        peak = jnp.max(peak, axis=1, keepdims=True)
        total = jnp.zeros((8, CHUNK), jnp.float32)
        summed = jnp.zeros((8, HEAD_DIM), jnp.float32)
        for step, score in enumerate(scores):
            first = part * per_part + step * CHUNK
            expo = jnp.exp2((score - peak) * EXPO)
            total = total + expo
            summed = summed + jnp.dot(
                expo.astype(jnp.bfloat16),
                v_vmem[first : first + CHUNK, :],
                preferred_element_type=jnp.float32,
            )
        return peak, jnp.sum(total, axis=1, keepdims=True), summed

    found = []
    scores = score_part(0)
    for part in range(1, PARTS):
        following = score_part(part)
        found.append(value_part(part - 1, scores))
        scores = following
    found.append(value_part(PARTS - 1, scores))
    top = functools.reduce(jnp.maximum, [peak for peak, _, _ in found])
    total = jnp.zeros((8, 1), jnp.float32)
    summed = jnp.zeros((8, HEAD_DIM), jnp.float32)
    for peak, part_total, part_summed in found:
        shrink = jnp.exp2((peak - top) * EXPO)
        total = total + part_total * shrink
        summed = summed + part_summed * shrink
    shape = (8, HEAD_DIM)
    return jnp.broadcast_to(top, shape), jnp.broadcast_to(total, shape), summed


def far_first(length, width):
    steps = [(z, y) for z in range(length) for y in range(width)]
    steps.sort(key=lambda s: -(min(s[0], length - s[0]) + min(s[1], width - s[1])))
    return steps


def kernel(
    q_hbm,
    k_hbm,
    v_hbm,
    w_hbm,
    size_hbm,
    start_hbm,
    length_hbm,
    owner_hbm,
    out_ref,
    q_ref,
    size_ref,
    start_ref,
    length_ref,
    owner_ref,
    k_vmem,
    k_turned,
    v_vmem,
    w_vmem,
    q_all,
    swap_out,
    swap_in,
    gathered,
    product,
    terms,
    load_sem,
    send_sem,
    recv_sem,
):
    me = lax.axis_index("seq")
    x = lax.axis_index("head")
    slots = k_hbm.shape[0]
    requests = size_ref.shape[0]
    base = (me // BLOCK) * BLOCK
    off = me - base
    core = me % 2
    chip = me // 2
    other = me + 1 - 2 * core
    chips = lax.axis_size("seq") // 2
    heads = lax.axis_size("head")
    half = w_hbm.shape[0] // 2

    columns = [
        pl.ds(pl.multiple_of((1 - core) * HEAD_DIM, HEAD_DIM), HEAD_DIM),
        pl.ds(pl.multiple_of(core * HEAD_DIM, HEAD_DIM), HEAD_DIM),
    ]
    loads = []
    for hbm, vmem in ((k_hbm, k_vmem), (v_hbm, v_vmem)):
        for turn in range(2):
            loads.append(
                pltpu.make_async_copy(
                    hbm.at[:, columns[turn]], vmem.at[turn], load_sem.at[len(loads)]
                )
            )
    mine = pl.ds(pl.multiple_of(core * half, half), half)
    theirs = pl.ds(pl.multiple_of((1 - core) * half, half), half)
    loads.append(pltpu.make_async_copy(w_hbm.at[mine], w_vmem.at[0], load_sem.at[4]))
    facts_in = [pltpu.make_async_copy(a, b, load_sem.at[5 + i]) for i, (a, b) in enumerate(((size_hbm, size_ref), (start_hbm, start_ref), (length_hbm, length_ref), (owner_hbm, owner_ref)))]
    query_in = pltpu.make_async_copy(q_hbm, q_ref, load_sem.at[9])
    query_in.start()

    z, y = chip // WIDTH, chip % WIDTH
    length = chips // WIDTH
    quarter = BLOCK // (2 * WIDTH)
    z_first = (z // quarter) * quarter

    def block_peers():
        for dz, dy in far_first(quarter, WIDTH):
            there = 2 * ((z_first + (z + dz) % quarter) * WIDTH + (y + dy) % WIDTH)
            yield there + 1 - core
            if (dz, dy) != (0, 0):
                yield there + core

    def plane_peers():
        for dz, dy in far_first(length, WIDTH):
            if (dz, dy) != (0, 0):
                yield 2 * (((z + dz) % length) * WIDTH + (y + dy) % WIDTH) + core

    other_half = ((me // BLOCK + 1) % 2) * quarter

    def other_half_peers():
        for dz, dy in far_first(quarter, WIDTH):
            yield 2 * ((other_half + (z + dz) % quarter) * WIDTH + (y + dy) % WIDTH) + core

    barrier = pltpu.get_barrier_semaphore()

    for peer in block_peers():
        pl.semaphore_signal(barrier, 1, device_id={"seq": peer}, device_id_type=MESH)
    for load in facts_in + loads:
        load.start()
    for peer in other_half_peers():
        pl.semaphore_signal(barrier, 1, device_id={"seq": peer}, device_id_type=MESH)
    for step in range(1, heads):
        across = (x + step) % heads
        for seq in (me, other):
            pl.semaphore_signal(
                barrier, 1, device_id={"seq": seq, "head": across}, device_id_type=MESH
            )

    query_in.wait()
    query = q_ref[...].astype(jnp.float32)
    rows = [query[:, h * HEAD_DIM : (h + 1) * HEAD_DIM] for h in range(16)]
    q_all[off] = jnp.concatenate(rows, axis=0).astype(jnp.bfloat16)
    pl.semaphore_wait(barrier, (BLOCK - 1) + BLOCK // 2 + 2 * (heads - 1))

    for peer in block_peers():
        pltpu.make_async_remote_copy(
            src_ref=q_all.at[off],
            dst_ref=q_all.at[off],
            send_sem=send_sem.at[0],
            recv_sem=recv_sem.at[0],
            device_id={"seq": peer},
            device_id_type=MESH,
        ).start()

    weight_copy = pltpu.make_async_remote_copy(
        src_ref=w_hbm.at[theirs],
        dst_ref=w_vmem.at[1],
        send_sem=send_sem.at[1],
        recv_sem=recv_sem.at[1],
        device_id={"seq": other},
        device_id_type=MESH,
    )

    weight_copy.start()
    for load in facts_in:
        load.wait()
    my_start = jnp.int32(0)
    my_length = jnp.int32(0)
    my_owner = jnp.int32(0)
    for r in range(requests):
        inside = (me >= start_ref[r]) & (me < start_ref[r] + size_ref[r])
        my_start = my_start + jnp.where(inside, start_ref[r], 0)
        my_length = my_length + jnp.where(inside, length_ref[r], 0)
        my_owner = my_owner + jnp.where(inside, owner_ref[r], 0)
    live = my_length - (me - my_start) * slots

    for turn in range(2):
        loads[turn].wait()
        for first in range(0, slots, TURN):
            rows = slice(first, first + TURN)
            k_turned[turn, :, rows] = k_vmem[turn, rows, :].T
    for load in loads[2:]:
        load.wait()
    queries_in = q_all.at[pl.ds(0, BLOCK - 1)]
    queries_copy = pltpu.make_async_remote_copy(
        src_ref=queries_in,
        dst_ref=queries_in,
        send_sem=send_sem.at[0],
        recv_sem=recv_sem.at[0],
        device_id={"seq": other},
        device_id_type=MESH,
    )
    queries_copy.wait_recv()
    query = q_all[lax.rem(my_owner, BLOCK)]
    first = core == 0

    theirs = attend(
        jnp.where(first, query[8:], query[:8]), k_turned.at[0], v_vmem.at[0], live, slots
    )
    for i in range(3):
        swap_out[8 * i : 8 * i + 8, :] = theirs[i]
    swap = pltpu.make_async_remote_copy(
        src_ref=swap_out,
        dst_ref=swap_in,
        send_sem=send_sem.at[2],
        recv_sem=recv_sem.at[2],
        device_id={"seq": other},
        device_id_type=MESH,
    )
    swap.start()
    top, total, summed = attend(
        jnp.where(first, query[:8], query[8:]), k_turned.at[1], v_vmem.at[1], live, slots
    )
    swap.wait_recv()
    their_top = swap_in[0:8, :]
    new_top = jnp.maximum(top, their_top)
    shrink = jnp.exp2((top - new_top) * EXPO)
    their_shrink = jnp.exp2((their_top - new_top) * EXPO)
    gathered[chip, 0:8, :] = summed * shrink + swap_in[16:24, :] * their_shrink
    total = total * shrink + swap_in[8:16, :] * their_shrink
    lane = lax.broadcasted_iota(jnp.int32, (8, HEAD_DIM), 1)
    row = lax.broadcasted_iota(jnp.int32, (8, HEAD_DIM), 0)
    facts = jnp.where(lane == row, new_top, 0.0) + jnp.where(lane == row + 8, total, 0.0)
    gathered[chip, 8:9, :] = jnp.sum(facts, axis=0, keepdims=True)

    for peer in plane_peers():
        pltpu.make_async_remote_copy(
            src_ref=gathered.at[chip, pl.ds(0, 9)],
            dst_ref=gathered.at[chip, pl.ds(0, 9)],
            send_sem=send_sem.at[3],
            recv_sem=recv_sem.at[3],
            device_id={"seq": peer},
            device_id_type=MESH,
        ).start()

    starts = jnp.zeros((8, chips), jnp.int32)
    ends = jnp.zeros((8, chips), jnp.int32)
    request = lax.broadcasted_iota(jnp.int32, (8, chips), 0)
    seq_of = 2 * lax.broadcasted_iota(jnp.int32, (8, chips), 1)
    for r in range(requests):
        starts = jnp.where(request == r, start_ref[r], starts)
        ends = jnp.where(request == r, start_ref[r] + size_ref[r], ends)
    member = ((seq_of >= starts) & (seq_of < ends)).astype(jnp.float32).astype(jnp.bfloat16)
    seq_down = 2 * lax.broadcasted_iota(jnp.int32, (chips, HEAD_DIM), 0)
    serves = [
        (seq_down >= start_ref[r]) & (seq_down < start_ref[r] + size_ref[r])
        for r in range(requests)
    ]

    gathered_in = gathered.at[pl.ds(0, chips - 1), pl.ds(0, 9)]
    gathered_copy = pltpu.make_async_remote_copy(
        src_ref=gathered_in,
        dst_ref=gathered_in,
        send_sem=send_sem.at[3],
        recv_sem=recv_sem.at[3],
        device_id={"seq": other},
        device_id_type=MESH,
    )
    gathered_copy.wait_recv()

    facts = gathered[:, 8, :]
    totals = pltpu.roll(facts, HEAD_DIM - 8, 1)
    tops = jnp.zeros((chips, HEAD_DIM), jnp.float32)
    for r in range(requests):
        top = jnp.max(jnp.where(serves[r], facts, NEG), axis=0, keepdims=True)
        tops = jnp.where(serves[r], top, tops)
    lane = lax.broadcasted_iota(jnp.int32, (chips, HEAD_DIM), 1)
    factor = jnp.exp2(jnp.where(lane < 8, (facts - tops) * EXPO, 0.0))
    scaled = factor * totals
    sums = jnp.ones((chips, HEAD_DIM), jnp.float32)
    for r in range(requests):
        total = jnp.sum(jnp.where(serves[r], scaled, 0.0), axis=0, keepdims=True)
        sums = jnp.where(serves[r], total, sums)
    factor = factor / sums
    pieces = [gathered[:, h, :] * factor[:, h : h + 1] for h in range(8)]
    weighted = jnp.concatenate(pieces, axis=1).astype(jnp.bfloat16)
    attended = jnp.dot(member, weighted, preferred_element_type=jnp.float32).astype(jnp.bfloat16)

    weight_copy.wait_recv()
    slot = 2 * x + core
    product[0] = jnp.dot(attended, w_vmem[1], preferred_element_type=jnp.float32)
    ours = jnp.dot(attended, w_vmem[0], preferred_element_type=jnp.float32)
    product[1] = ours
    terms[slot] = ours

    def final(which, seq, across):
        return pltpu.make_async_remote_copy(
            src_ref=product.at[which],
            dst_ref=terms.at[slot],
            send_sem=send_sem.at[4],
            recv_sem=recv_sem.at[4],
            device_id={"seq": seq, "head": across},
            device_id_type=MESH,
        )

    for step in (2, 1, 3):
        final(0, other, (x + step) % heads).start()
        final(1, me, (x + step) % heads).start()
    final(0, other, x).start()

    terms_in = terms.at[pl.ds(0, 2 * heads - 1)]
    terms_copy = pltpu.make_async_remote_copy(
        src_ref=terms_in,
        dst_ref=terms_in,
        send_sem=send_sem.at[4],
        recv_sem=recv_sem.at[4],
        device_id={"seq": other},
        device_id_type=MESH,
    )
    queries_copy.wait_send()
    weight_copy.wait_send()
    swap.wait_send()
    gathered_copy.wait_send()
    terms_copy.wait_recv()
    out = terms[0]
    for i in range(1, 2 * heads):
        out = out + terms[i]
    out_ref[...] = out[:requests].astype(jnp.bfloat16)
    terms_copy.wait_send()


def per_device(queries, k_cache, v_cache, o_weight, group_size, group_start, cache_len, owner):
    requests = group_size.shape[0]
    slots, width = k_cache.shape
    rows, columns = o_weight.shape
    chips = lax.axis_size("seq") // 2
    heads = lax.axis_size("head")
    hbm = pl.BlockSpec(memory_space=pl.ANY)
    vmem = pl.BlockSpec(memory_space=pltpu.VMEM)
    smem = pl.BlockSpec(memory_space=pltpu.SMEM)
    return pl.pallas_call(
        kernel,
        out_shape=jax.ShapeDtypeStruct((requests, columns), jnp.bfloat16),
        in_specs=[hbm, hbm, hbm, hbm, hbm, hbm, hbm, hbm],
        out_specs=vmem,
        scratch_shapes=[
            pltpu.VMEM(queries.shape, jnp.bfloat16),
            pltpu.SMEM((requests,), jnp.int32),
            pltpu.SMEM((requests,), jnp.int32),
            pltpu.SMEM((requests,), jnp.int32),
            pltpu.SMEM((requests,), jnp.int32),
            pltpu.VMEM((2, slots, width // 2), jnp.bfloat16),
            pltpu.VMEM((2, width // 2, slots), jnp.bfloat16),
            pltpu.VMEM((2, slots, width // 2), jnp.bfloat16),
            pltpu.VMEM((2, rows // 2, columns), jnp.bfloat16),
            pltpu.VMEM((BLOCK, 16, HEAD_DIM), jnp.bfloat16),
            pltpu.VMEM((24, HEAD_DIM), jnp.float32),
            pltpu.VMEM((24, HEAD_DIM), jnp.float32),
            pltpu.VMEM((chips, 16, HEAD_DIM), jnp.float32),
            pltpu.VMEM((2, 8, columns), jnp.float32),
            pltpu.VMEM((2 * heads, 8, columns), jnp.float32),
            pltpu.SemaphoreType.DMA((10,)),
            pltpu.SemaphoreType.DMA((5,)),
            pltpu.SemaphoreType.DMA((5,)),
        ],
        compiler_params=pltpu.CompilerParams(
            collective_id=0, has_side_effects=True, vmem_limit_bytes=56 * 1024 * 1024
        ),
    )(queries, k_cache, v_cache, o_weight, group_size, group_start, cache_len, owner)


def solution(mesh):
    in_specs = (
        P("seq", "head"),
        P("seq", "head"),
        P("seq", "head"),
        P("head", "seq"),
        P(),
        P(),
        P(),
        P(),
    )
    out_specs = P(None, "seq")
    return jax.shard_map(
        per_device, mesh=mesh, in_specs=in_specs, out_specs=out_specs, check_vma=False
    )
```

```python
import functools

import jax
import jax.numpy as jnp
from jax import lax
from jax.experimental import pallas as pl
from jax.experimental.pallas import tpu as pltpu
from jax.sharding import PartitionSpec as P

HEAD_DIM = 128
MESH = pl.DeviceIdType.MESH
LOG2E = 1.4426950408889634
SCALE = HEAD_DIM ** (-0.5)
EXPO = SCALE * LOG2E
NEG = -1e30 / SCALE
BLOCK = 32
WIDTH = 4
PARTS = 4
CHUNK = 1024
TURN = 256


def attend(query, k_turned, v_vmem, live, slots):
    lane = lax.broadcasted_iota(jnp.int32, (8, CHUNK), 1)
    per_part = slots // PARTS

    def score_part(part):
        scores = []
        for first in range(part * per_part, (part + 1) * per_part, CHUNK):
            keys = k_turned[:, first : first + CHUNK]
            score = jnp.dot(query, keys, preferred_element_type=jnp.float32)
            scores.append(jnp.where(lane < live - first, score, NEG))
        return scores

    def value_part(part, scores):
        peak = functools.reduce(jnp.maximum, scores)
        peak = jnp.max(peak, axis=1, keepdims=True)
        total = jnp.zeros((8, CHUNK), jnp.float32)
        summed = jnp.zeros((8, HEAD_DIM), jnp.float32)
        for step, score in enumerate(scores):
            first = part * per_part + step * CHUNK
            expo = jnp.exp2((score - peak) * EXPO)
            total = total + expo
            summed = summed + jnp.dot(
                expo.astype(jnp.bfloat16),
                v_vmem[first : first + CHUNK, :],
                preferred_element_type=jnp.float32,
            )
        return peak, jnp.sum(total, axis=1, keepdims=True), summed

    found = []
    scores = score_part(0)
    for part in range(1, PARTS):
        following = score_part(part)
        found.append(value_part(part - 1, scores))
        scores = following
    found.append(value_part(PARTS - 1, scores))
    top = functools.reduce(jnp.maximum, [peak for peak, _, _ in found])
    total = jnp.zeros((8, 1), jnp.float32)
    summed = jnp.zeros((8, HEAD_DIM), jnp.float32)
    for peak, part_total, part_summed in found:
        shrink = jnp.exp2((peak - top) * EXPO)
        total = total + part_total * shrink
        summed = summed + part_summed * shrink
    shape = (8, HEAD_DIM)
    return jnp.broadcast_to(top, shape), jnp.broadcast_to(total, shape), summed


def far_first(length, width):
    steps = [(z, y) for z in range(length) for y in range(width)]
    steps.sort(key=lambda s: -(min(s[0], length - s[0]) + min(s[1], width - s[1])))
    return steps


def kernel(
    q_hbm,
    k_hbm,
    v_hbm,
    w_hbm,
    size_hbm,
    start_hbm,
    length_hbm,
    owner_hbm,
    terms,
    q_ref,
    size_ref,
    start_ref,
    length_ref,
    owner_ref,
    k_vmem,
    k_turned,
    v_vmem,
    w_vmem,
    q_all,
    swap_out,
    swap_in,
    gathered,
    product,
    load_sem,
    send_sem,
    recv_sem,
    late_sem,
):
    me = lax.axis_index("seq")
    x = lax.axis_index("head")
    slots = k_hbm.shape[0]
    requests = size_ref.shape[0]
    base = (me // BLOCK) * BLOCK
    off = me - base
    core = me % 2
    chip = me // 2
    other = me + 1 - 2 * core
    chips = lax.axis_size("seq") // 2
    heads = lax.axis_size("head")
    half = w_hbm.shape[0] // 2

    columns = [
        pl.ds(pl.multiple_of((1 - core) * HEAD_DIM, HEAD_DIM), HEAD_DIM),
        pl.ds(pl.multiple_of(core * HEAD_DIM, HEAD_DIM), HEAD_DIM),
    ]
    loads = []
    for hbm, vmem in ((k_hbm, k_vmem), (v_hbm, v_vmem)):
        for turn in range(2):
            loads.append(
                pltpu.make_async_copy(
                    hbm.at[:, columns[turn]], vmem.at[turn], load_sem.at[len(loads)]
                )
            )
    mine = pl.ds(pl.multiple_of(core * half, half), half)
    theirs = pl.ds(pl.multiple_of((1 - core) * half, half), half)
    loads.append(pltpu.make_async_copy(w_hbm.at[mine], w_vmem.at[0], load_sem.at[4]))
    facts_in = [pltpu.make_async_copy(a, b, load_sem.at[5 + i]) for i, (a, b) in enumerate(((size_hbm, size_ref), (start_hbm, start_ref), (length_hbm, length_ref), (owner_hbm, owner_ref)))]
    query_in = pltpu.make_async_copy(q_hbm, q_ref, load_sem.at[9])
    query_in.start()

    z, y = chip // WIDTH, chip % WIDTH
    length = chips // WIDTH
    quarter = BLOCK // (2 * WIDTH)
    z_first = (z // quarter) * quarter

    early = me < BLOCK

    def block_peers():
        for dz, dy in far_first(quarter, WIDTH):
            there = 2 * ((z_first + (z + dz) % quarter) * WIDTH + (y + dy) % WIDTH)
            yield there + 1 - core
            if (dz, dy) != (0, 0):
                yield there + core

    def same_core_peers():
        for dz, dy in far_first(quarter, WIDTH):
            if (dz, dy) != (0, 0):
                yield 2 * ((z_first + (z + dz) % quarter) * WIDTH + (y + dy) % WIDTH) + core

    def plane_peers():
        for dz, dy in far_first(length, WIDTH):
            if (dz, dy) != (0, 0):
                yield 2 * (((z + dz) % length) * WIDTH + (y + dy) % WIDTH) + core

    other_half = ((me // BLOCK + 1) % 2) * quarter

    def other_half_peers():
        for dz, dy in far_first(quarter, WIDTH):
            yield 2 * ((other_half + (z + dz) % quarter) * WIDTH + (y + dy) % WIDTH) + core

    barrier = pltpu.get_barrier_semaphore()

    for peer in block_peers():
        pl.semaphore_signal(barrier, 1, device_id={"seq": peer}, device_id_type=MESH)
    for load in facts_in + loads:
        load.start()

    @pl.when(early)
    def _():
        for peer in other_half_peers():
            pl.semaphore_signal(barrier, 1, device_id={"seq": peer}, device_id_type=MESH)

    for step in range(1, heads):
        across = (x + step) % heads
        for seq in (me, other):
            pl.semaphore_signal(
                barrier, 1, device_id={"seq": seq, "head": across}, device_id_type=MESH
            )

    query_in.wait()
    query = q_ref[...].astype(jnp.float32)
    rows = [query[:, h * HEAD_DIM : (h + 1) * HEAD_DIM] for h in range(16)]
    q_all[off] = jnp.concatenate(rows, axis=0).astype(jnp.bfloat16)
    @pl.when(early)
    def _():
        pl.semaphore_wait(barrier, (BLOCK - 1) + 2 * (heads - 1))

    @pl.when(jnp.logical_not(early))
    def _():
        pl.semaphore_wait(barrier, (BLOCK - 1) + BLOCK // 2 + 2 * (heads - 1))


    for peer in block_peers():
        pltpu.make_async_remote_copy(
            src_ref=q_all.at[off],
            dst_ref=q_all.at[off],
            send_sem=send_sem.at[0],
            recv_sem=recv_sem.at[0],
            device_id={"seq": peer},
            device_id_type=MESH,
        ).start()

    weight_copy = pltpu.make_async_remote_copy(
        src_ref=w_hbm.at[theirs],
        dst_ref=w_vmem.at[1],
        send_sem=send_sem.at[1],
        recv_sem=recv_sem.at[1],
        device_id={"seq": other},
        device_id_type=MESH,
    )

    weight_copy.start()

    @pl.when(jnp.logical_not(early))
    def _():
        for peer in other_half_peers():
            pl.semaphore_signal(late_sem, 1, device_id={"seq": peer}, device_id_type=MESH)

    for load in facts_in:
        load.wait()
    my_start = jnp.int32(0)
    my_length = jnp.int32(0)
    my_owner = jnp.int32(0)
    for r in range(requests):
        inside = (me >= start_ref[r]) & (me < start_ref[r] + size_ref[r])
        my_start = my_start + jnp.where(inside, start_ref[r], 0)
        my_length = my_length + jnp.where(inside, length_ref[r], 0)
        my_owner = my_owner + jnp.where(inside, owner_ref[r], 0)
    live = my_length - (me - my_start) * slots

    for turn in range(2):
        loads[turn].wait()
        for first in range(0, slots, TURN):
            rows = slice(first, first + TURN)
            k_turned[turn, :, rows] = k_vmem[turn, rows, :].T
    for load in loads[2:]:
        load.wait()
    queries_in = q_all.at[pl.ds(0, BLOCK - 1)]
    queries_copy = pltpu.make_async_remote_copy(
        src_ref=queries_in,
        dst_ref=queries_in,
        send_sem=send_sem.at[0],
        recv_sem=recv_sem.at[0],
        device_id={"seq": other},
        device_id_type=MESH,
    )
    queries_copy.wait_recv()
    query = q_all[lax.rem(my_owner, BLOCK)]
    first = core == 0

    theirs = attend(
        jnp.where(first, query[8:], query[:8]), k_turned.at[0], v_vmem.at[0], live, slots
    )
    for i in range(3):
        swap_out[8 * i : 8 * i + 8, :] = theirs[i]
    swap = pltpu.make_async_remote_copy(
        src_ref=swap_out,
        dst_ref=swap_in,
        send_sem=send_sem.at[2],
        recv_sem=recv_sem.at[2],
        device_id={"seq": other},
        device_id_type=MESH,
    )
    swap.start()
    top, total, summed = attend(
        jnp.where(first, query[:8], query[8:]), k_turned.at[1], v_vmem.at[1], live, slots
    )
    swap.wait_recv()
    their_top = swap_in[0:8, :]
    new_top = jnp.maximum(top, their_top)
    shrink = jnp.exp2((top - new_top) * EXPO)
    their_shrink = jnp.exp2((their_top - new_top) * EXPO)
    gathered[chip, 0:8, :] = summed * shrink + swap_in[16:24, :] * their_shrink
    total = total * shrink + swap_in[8:16, :] * their_shrink
    lane = lax.broadcasted_iota(jnp.int32, (8, HEAD_DIM), 1)
    row = lax.broadcasted_iota(jnp.int32, (8, HEAD_DIM), 0)
    facts = jnp.where(lane == row, new_top, 0.0) + jnp.where(lane == row + 8, total, 0.0)
    gathered[chip, 8:9, :] = jnp.sum(facts, axis=0, keepdims=True)

    def send_gathered(peer):
        pltpu.make_async_remote_copy(
            src_ref=gathered.at[chip, pl.ds(0, 9)],
            dst_ref=gathered.at[chip, pl.ds(0, 9)],
            send_sem=send_sem.at[3],
            recv_sem=recv_sem.at[3],
            device_id={"seq": peer},
            device_id_type=MESH,
        ).start()

    @pl.when(early)
    def _():
        for peer in same_core_peers():
            send_gathered(peer)
        pl.semaphore_wait(late_sem, BLOCK // 2)
        for peer in other_half_peers():
            send_gathered(peer)

    @pl.when(jnp.logical_not(early))
    def _():
        for there in range(BLOCK // 2):
            send_gathered(2 * there + core)
        for peer in same_core_peers():
            send_gathered(peer)

    starts = jnp.zeros((8, chips), jnp.int32)
    ends = jnp.zeros((8, chips), jnp.int32)
    request = lax.broadcasted_iota(jnp.int32, (8, chips), 0)
    seq_of = 2 * lax.broadcasted_iota(jnp.int32, (8, chips), 1)
    for r in range(requests):
        starts = jnp.where(request == r, start_ref[r], starts)
        ends = jnp.where(request == r, start_ref[r] + size_ref[r], ends)
    member = ((seq_of >= starts) & (seq_of < ends)).astype(jnp.float32).astype(jnp.bfloat16)
    seq_down = 2 * lax.broadcasted_iota(jnp.int32, (chips, HEAD_DIM), 0)
    serves = [
        (seq_down >= start_ref[r]) & (seq_down < start_ref[r] + size_ref[r])
        for r in range(requests)
    ]

    gathered_in = gathered.at[pl.ds(0, chips - 1), pl.ds(0, 9)]
    gathered_copy = pltpu.make_async_remote_copy(
        src_ref=gathered_in,
        dst_ref=gathered_in,
        send_sem=send_sem.at[3],
        recv_sem=recv_sem.at[3],
        device_id={"seq": other},
        device_id_type=MESH,
    )
    gathered_copy.wait_recv()

    facts = gathered[:, 8, :]
    totals = pltpu.roll(facts, HEAD_DIM - 8, 1)
    tops = jnp.zeros((chips, HEAD_DIM), jnp.float32)
    for r in range(requests):
        top = jnp.max(jnp.where(serves[r], facts, NEG), axis=0, keepdims=True)
        tops = jnp.where(serves[r], top, tops)
    lane = lax.broadcasted_iota(jnp.int32, (chips, HEAD_DIM), 1)
    factor = jnp.exp2(jnp.where(lane < 8, (facts - tops) * EXPO, 0.0))
    scaled = factor * totals
    sums = jnp.ones((chips, HEAD_DIM), jnp.float32)
    for r in range(requests):
        total = jnp.sum(jnp.where(serves[r], scaled, 0.0), axis=0, keepdims=True)
        sums = jnp.where(serves[r], total, sums)
    factor = factor / sums
    pieces = [gathered[:, h, :] * factor[:, h : h + 1] for h in range(8)]
    weighted = jnp.concatenate(pieces, axis=1).astype(jnp.bfloat16)
    attended = jnp.dot(member, weighted, preferred_element_type=jnp.float32).astype(jnp.bfloat16)

    weight_copy.wait_recv()
    slot = 2 * x + core
    product[0] = jnp.dot(attended, w_vmem[1], preferred_element_type=jnp.float32)
    ours = jnp.dot(attended, w_vmem[0], preferred_element_type=jnp.float32)
    product[1] = ours
    own_copy = pltpu.make_async_copy(product.at[1], terms.at[slot], load_sem.at[10])

    def final(which, seq, across):
        return pltpu.make_async_remote_copy(
            src_ref=product.at[which],
            dst_ref=terms.at[slot],
            send_sem=send_sem.at[4],
            recv_sem=recv_sem.at[4],
            device_id={"seq": seq, "head": across},
            device_id_type=MESH,
        )

    for step in (2, 1, 3):
        final(0, other, (x + step) % heads).start()
        final(1, me, (x + step) % heads).start()
    final(0, other, x).start()
    own_copy.start()

    terms_in = terms.at[pl.ds(0, 2 * heads - 1)]
    terms_copy = pltpu.make_async_remote_copy(
        src_ref=terms_in,
        dst_ref=terms_in,
        send_sem=send_sem.at[4],
        recv_sem=recv_sem.at[4],
        device_id={"seq": other},
        device_id_type=MESH,
    )
    queries_copy.wait_send()
    weight_copy.wait_send()
    swap.wait_send()
    gathered_copy.wait_send()
    terms_copy.wait_recv()
    own_copy.wait()
    terms_copy.wait_send()


def per_device(queries, k_cache, v_cache, o_weight, group_size, group_start, cache_len, owner):
    requests = group_size.shape[0]
    slots, width = k_cache.shape
    rows, columns = o_weight.shape
    chips = lax.axis_size("seq") // 2
    heads = lax.axis_size("head")
    hbm = pl.BlockSpec(memory_space=pl.ANY)
    vmem = pl.BlockSpec(memory_space=pltpu.VMEM)
    smem = pl.BlockSpec(memory_space=pltpu.SMEM)
    terms = pl.pallas_call(
        kernel,
        out_shape=jax.ShapeDtypeStruct((2 * heads, 8, columns), jnp.float32),
        in_specs=[hbm, hbm, hbm, hbm, hbm, hbm, hbm, hbm],
        out_specs=hbm,
        scratch_shapes=[
            pltpu.VMEM(queries.shape, jnp.bfloat16),
            pltpu.SMEM((requests,), jnp.int32),
            pltpu.SMEM((requests,), jnp.int32),
            pltpu.SMEM((requests,), jnp.int32),
            pltpu.SMEM((requests,), jnp.int32),
            pltpu.VMEM((2, slots, width // 2), jnp.bfloat16),
            pltpu.VMEM((2, width // 2, slots), jnp.bfloat16),
            pltpu.VMEM((2, slots, width // 2), jnp.bfloat16),
            pltpu.VMEM((2, rows // 2, columns), jnp.bfloat16),
            pltpu.VMEM((BLOCK, 16, HEAD_DIM), jnp.bfloat16),
            pltpu.VMEM((24, HEAD_DIM), jnp.float32),
            pltpu.VMEM((24, HEAD_DIM), jnp.float32),
            pltpu.VMEM((chips, 16, HEAD_DIM), jnp.float32),
            pltpu.VMEM((2, 8, columns), jnp.float32),
            pltpu.SemaphoreType.DMA((11,)),
            pltpu.SemaphoreType.DMA((5,)),
            pltpu.SemaphoreType.DMA((5,)),
            pltpu.SemaphoreType.REGULAR,
        ],
        compiler_params=pltpu.CompilerParams(
            collective_id=0, has_side_effects=True, vmem_limit_bytes=56 * 1024 * 1024
        ),
    )(queries, k_cache, v_cache, o_weight, group_size, group_start, cache_len, owner)
    return jnp.sum(terms, axis=0)[:requests].astype(jnp.bfloat16)


def solution(mesh):
    in_specs = (
        P("seq", "head"),
        P("seq", "head"),
        P("seq", "head"),
        P("head", "seq"),
        P(),
        P(),
        P(),
        P(),
    )
    out_specs = P(None, "seq")
    return jax.shard_map(
        per_device, mesh=mesh, in_specs=in_specs, out_specs=out_specs, check_vma=False
    )
```

```python
import functools

import jax
import jax.numpy as jnp
from jax import lax
from jax.experimental import pallas as pl
from jax.experimental.pallas import tpu as pltpu
from jax.sharding import PartitionSpec as P

HEAD_DIM = 128
MESH = pl.DeviceIdType.MESH
LOG2E = 1.4426950408889634
SCALE = HEAD_DIM ** (-0.5)
EXPO = SCALE * LOG2E
NEG = -1e30 / SCALE
BLOCK = 32
WIDTH = 4
PARTS = 4
CHUNK = 1024
TURN = 256


def attend(query, k_turned, v_vmem, live, slots):
    lane = lax.broadcasted_iota(jnp.int32, (8, CHUNK), 1)
    per_part = slots // PARTS

    def score_part(part):
        scores = []
        for first in range(part * per_part, (part + 1) * per_part, CHUNK):
            keys = k_turned[:, first : first + CHUNK]
            score = jnp.dot(query, keys, preferred_element_type=jnp.float32)
            scores.append(jnp.where(lane < live - first, score, NEG))
        return scores

    def value_part(part, scores):
        peak = functools.reduce(jnp.maximum, scores)
        peak = jnp.max(peak, axis=1, keepdims=True)
        total = jnp.zeros((8, CHUNK), jnp.float32)
        summed = jnp.zeros((8, HEAD_DIM), jnp.float32)
        for step, score in enumerate(scores):
            first = part * per_part + step * CHUNK
            expo = jnp.exp2((score - peak) * EXPO)
            total = total + expo
            summed = summed + jnp.dot(
                expo.astype(jnp.bfloat16),
                v_vmem[first : first + CHUNK, :],
                preferred_element_type=jnp.float32,
            )
        return peak, jnp.sum(total, axis=1, keepdims=True), summed

    found = []
    scores = score_part(0)
    for part in range(1, PARTS):
        following = score_part(part)
        found.append(value_part(part - 1, scores))
        scores = following
    found.append(value_part(PARTS - 1, scores))
    top = functools.reduce(jnp.maximum, [peak for peak, _, _ in found])
    total = jnp.zeros((8, 1), jnp.float32)
    summed = jnp.zeros((8, HEAD_DIM), jnp.float32)
    for peak, part_total, part_summed in found:
        shrink = jnp.exp2((peak - top) * EXPO)
        total = total + part_total * shrink
        summed = summed + part_summed * shrink
    shape = (8, HEAD_DIM)
    return jnp.broadcast_to(top, shape), jnp.broadcast_to(total, shape), summed


def far_first(length, width):
    steps = [(z, y) for z in range(length) for y in range(width)]
    steps.sort(key=lambda s: -(min(s[0], length - s[0]) + min(s[1], width - s[1])))
    return steps


def kernel(
    q_hbm,
    k_hbm,
    v_hbm,
    w_hbm,
    size_hbm,
    start_hbm,
    length_hbm,
    owner_hbm,
    terms,
    q_ref,
    size_ref,
    start_ref,
    length_ref,
    owner_ref,
    k_vmem,
    k_turned,
    v_vmem,
    w_vmem,
    q_all,
    swap_out,
    swap_in,
    gathered,
    product,
    load_sem,
    send_sem,
    recv_sem,
    late_sem,
):
    me = lax.axis_index("seq")
    x = lax.axis_index("head")
    slots = k_hbm.shape[0]
    requests = size_ref.shape[0]
    base = (me // BLOCK) * BLOCK
    off = me - base
    core = me % 2
    chip = me // 2
    other = me + 1 - 2 * core
    chips = lax.axis_size("seq") // 2
    heads = lax.axis_size("head")
    half = w_hbm.shape[0] // 2

    columns = [
        pl.ds(pl.multiple_of((1 - core) * HEAD_DIM, HEAD_DIM), HEAD_DIM),
        pl.ds(pl.multiple_of(core * HEAD_DIM, HEAD_DIM), HEAD_DIM),
    ]
    loads = []
    for hbm, vmem in ((k_hbm, k_vmem), (v_hbm, v_vmem)):
        for turn in range(2):
            loads.append(
                pltpu.make_async_copy(
                    hbm.at[:, columns[turn]], vmem.at[turn], load_sem.at[len(loads)]
                )
            )
    mine = pl.ds(pl.multiple_of(core * half, half), half)
    theirs = pl.ds(pl.multiple_of((1 - core) * half, half), half)
    loads.append(pltpu.make_async_copy(w_hbm.at[mine], w_vmem.at[0], load_sem.at[4]))
    facts_in = [pltpu.make_async_copy(a, b, load_sem.at[5 + i]) for i, (a, b) in enumerate(((size_hbm, size_ref), (start_hbm, start_ref), (length_hbm, length_ref), (owner_hbm, owner_ref)))]
    query_in = pltpu.make_async_copy(q_hbm, q_ref, load_sem.at[9])
    query_in.start()

    z, y = chip // WIDTH, chip % WIDTH
    quarter = BLOCK // (2 * WIDTH)
    z_first = (z // quarter) * quarter

    early = me < BLOCK

    z_own = z % quarter
    z_there = (z_own, z_own + 1 - 2 * (z_own % 2), (z_own + 2) % quarter, quarter - 1 - z_own)
    block_steps = [(way, dy) for way in range(quarter) for dy in range(WIDTH)]
    block_steps.sort(key=lambda s: -(s[0] + min(s[1], WIDTH - s[1])))

    def block_peers():
        for way, dy in block_steps:
            there = 2 * ((z_first + z_there[way]) * WIDTH + (y + dy) % WIDTH)
            yield there + 1 - core
            if (way, dy) != (0, 0):
                yield there + core

    def same_core_peers():
        for way, dy in block_steps:
            if (way, dy) != (0, 0):
                yield 2 * ((z_first + z_there[way]) * WIDTH + (y + dy) % WIDTH) + core

    other_half = ((me // BLOCK + 1) % 2) * quarter

    def other_half_peers():
        for dz, dy in far_first(quarter, WIDTH):
            yield 2 * ((other_half + (z + dz) % quarter) * WIDTH + (y + dy) % WIDTH) + core

    barrier = pltpu.get_barrier_semaphore()

    for peer in block_peers():
        pl.semaphore_signal(barrier, 1, device_id={"seq": peer}, device_id_type=MESH)
    for load in facts_in + loads:
        load.start()

    @pl.when(early)
    def _():
        for peer in other_half_peers():
            pl.semaphore_signal(barrier, 1, device_id={"seq": peer}, device_id_type=MESH)

    for step in range(1, heads):
        across = (x + step) % heads
        for seq in (me, other):
            pl.semaphore_signal(
                barrier, 1, device_id={"seq": seq, "head": across}, device_id_type=MESH
            )

    query_in.wait()
    query = q_ref[...].astype(jnp.float32)
    rows = [query[:, h * HEAD_DIM : (h + 1) * HEAD_DIM] for h in range(16)]
    q_all[off] = jnp.concatenate(rows, axis=0).astype(jnp.bfloat16)
    @pl.when(early)
    def _():
        pl.semaphore_wait(barrier, (BLOCK - 1) + 2 * (heads - 1))

    @pl.when(jnp.logical_not(early))
    def _():
        pl.semaphore_wait(barrier, (BLOCK - 1) + BLOCK // 2 + 2 * (heads - 1))


    for peer in block_peers():
        pltpu.make_async_remote_copy(
            src_ref=q_all.at[off],
            dst_ref=q_all.at[off],
            send_sem=send_sem.at[0],
            recv_sem=recv_sem.at[0],
            device_id={"seq": peer},
            device_id_type=MESH,
        ).start()

    weight_copy = pltpu.make_async_remote_copy(
        src_ref=w_hbm.at[theirs],
        dst_ref=w_vmem.at[1],
        send_sem=send_sem.at[1],
        recv_sem=recv_sem.at[1],
        device_id={"seq": other},
        device_id_type=MESH,
    )

    weight_copy.start()

    @pl.when(jnp.logical_not(early))
    def _():
        for peer in other_half_peers():
            pl.semaphore_signal(late_sem, 1, device_id={"seq": peer}, device_id_type=MESH)

    for load in facts_in:
        load.wait()
    my_start = jnp.int32(0)
    my_length = jnp.int32(0)
    my_owner = jnp.int32(0)
    for r in range(requests):
        inside = (me >= start_ref[r]) & (me < start_ref[r] + size_ref[r])
        my_start = my_start + jnp.where(inside, start_ref[r], 0)
        my_length = my_length + jnp.where(inside, length_ref[r], 0)
        my_owner = my_owner + jnp.where(inside, owner_ref[r], 0)
    live = my_length - (me - my_start) * slots

    for turn in range(2):
        loads[turn].wait()
        for first in range(0, slots, TURN):
            rows = slice(first, first + TURN)
            k_turned[turn, :, rows] = k_vmem[turn, rows, :].T
    for load in loads[2:]:
        load.wait()
    queries_in = q_all.at[pl.ds(0, BLOCK - 1)]
    queries_copy = pltpu.make_async_remote_copy(
        src_ref=queries_in,
        dst_ref=queries_in,
        send_sem=send_sem.at[0],
        recv_sem=recv_sem.at[0],
        device_id={"seq": other},
        device_id_type=MESH,
    )
    queries_copy.wait_recv()
    query = q_all[lax.rem(my_owner, BLOCK)]
    first = core == 0

    theirs = attend(
        jnp.where(first, query[8:], query[:8]), k_turned.at[0], v_vmem.at[0], live, slots
    )
    for i in range(3):
        swap_out[8 * i : 8 * i + 8, :] = theirs[i]
    swap = pltpu.make_async_remote_copy(
        src_ref=swap_out,
        dst_ref=swap_in,
        send_sem=send_sem.at[2],
        recv_sem=recv_sem.at[2],
        device_id={"seq": other},
        device_id_type=MESH,
    )
    swap.start()
    top, total, summed = attend(
        jnp.where(first, query[:8], query[8:]), k_turned.at[1], v_vmem.at[1], live, slots
    )
    swap.wait_recv()
    their_top = swap_in[0:8, :]
    new_top = jnp.maximum(top, their_top)
    shrink = jnp.exp2((top - new_top) * EXPO)
    their_shrink = jnp.exp2((their_top - new_top) * EXPO)
    gathered[chip, 0:8, :] = summed * shrink + swap_in[16:24, :] * their_shrink
    total = total * shrink + swap_in[8:16, :] * their_shrink
    lane = lax.broadcasted_iota(jnp.int32, (8, HEAD_DIM), 1)
    row = lax.broadcasted_iota(jnp.int32, (8, HEAD_DIM), 0)
    facts = jnp.where(lane == row, new_top, 0.0) + jnp.where(lane == row + 8, total, 0.0)
    gathered[chip, 8:9, :] = jnp.sum(facts, axis=0, keepdims=True)

    def send_gathered(peer):
        pltpu.make_async_remote_copy(
            src_ref=gathered.at[chip, pl.ds(0, 9)],
            dst_ref=gathered.at[chip, pl.ds(0, 9)],
            send_sem=send_sem.at[3],
            recv_sem=recv_sem.at[3],
            device_id={"seq": peer},
            device_id_type=MESH,
        ).start()

    @pl.when(early)
    def _():
        for peer in same_core_peers():
            send_gathered(peer)
        pl.semaphore_wait(late_sem, BLOCK // 2)
        for peer in other_half_peers():
            send_gathered(peer)

    @pl.when(jnp.logical_not(early))
    def _():
        for there in range(BLOCK // 2):
            send_gathered(2 * there + core)
        for peer in same_core_peers():
            send_gathered(peer)

    starts = jnp.zeros((8, chips), jnp.int32)
    ends = jnp.zeros((8, chips), jnp.int32)
    request = lax.broadcasted_iota(jnp.int32, (8, chips), 0)
    seq_of = 2 * lax.broadcasted_iota(jnp.int32, (8, chips), 1)
    for r in range(requests):
        starts = jnp.where(request == r, start_ref[r], starts)
        ends = jnp.where(request == r, start_ref[r] + size_ref[r], ends)
    member = ((seq_of >= starts) & (seq_of < ends)).astype(jnp.float32).astype(jnp.bfloat16)
    seq_down = 2 * lax.broadcasted_iota(jnp.int32, (chips, HEAD_DIM), 0)
    serves = [
        (seq_down >= start_ref[r]) & (seq_down < start_ref[r] + size_ref[r])
        for r in range(requests)
    ]

    gathered_in = gathered.at[pl.ds(0, chips - 1), pl.ds(0, 9)]
    gathered_copy = pltpu.make_async_remote_copy(
        src_ref=gathered_in,
        dst_ref=gathered_in,
        send_sem=send_sem.at[3],
        recv_sem=recv_sem.at[3],
        device_id={"seq": other},
        device_id_type=MESH,
    )
    gathered_copy.wait_recv()

    facts = gathered[:, 8, :]
    totals = pltpu.roll(facts, HEAD_DIM - 8, 1)
    tops = jnp.zeros((chips, HEAD_DIM), jnp.float32)
    for r in range(requests):
        top = jnp.max(jnp.where(serves[r], facts, NEG), axis=0, keepdims=True)
        tops = jnp.where(serves[r], top, tops)
    lane = lax.broadcasted_iota(jnp.int32, (chips, HEAD_DIM), 1)
    factor = jnp.exp2(jnp.where(lane < 8, (facts - tops) * EXPO, 0.0))
    scaled = factor * totals
    sums = jnp.ones((chips, HEAD_DIM), jnp.float32)
    for r in range(requests):
        total = jnp.sum(jnp.where(serves[r], scaled, 0.0), axis=0, keepdims=True)
        sums = jnp.where(serves[r], total, sums)
    factor = factor / sums
    pieces = [gathered[:, h, :] * factor[:, h : h + 1] for h in range(8)]
    weighted = jnp.concatenate(pieces, axis=1).astype(jnp.bfloat16)
    attended = jnp.dot(member, weighted, preferred_element_type=jnp.float32).astype(jnp.bfloat16)

    weight_copy.wait_recv()
    slot = 2 * x + core

    def final(which, seq, across):
        return pltpu.make_async_remote_copy(
            src_ref=product.at[which],
            dst_ref=terms.at[slot],
            send_sem=send_sem.at[4],
            recv_sem=recv_sem.at[4],
            device_id={"seq": seq, "head": across},
            device_id_type=MESH,
        )

    own_copy = pltpu.make_async_copy(product.at[core], terms.at[slot], load_sem.at[10])
    for to_core in (1, 0):
        which = (core + to_core) % 2
        product[to_core] = jnp.dot(
            attended, w_vmem[which], preferred_element_type=jnp.float32
        )
        for across in range(heads):

            @pl.when(jnp.logical_or(across != x, to_core != core))
            def _():
                final(to_core, me - core + to_core, across).start()

    own_copy.start()

    terms_in = terms.at[pl.ds(0, 2 * heads - 1)]
    terms_copy = pltpu.make_async_remote_copy(
        src_ref=terms_in,
        dst_ref=terms_in,
        send_sem=send_sem.at[4],
        recv_sem=recv_sem.at[4],
        device_id={"seq": other},
        device_id_type=MESH,
    )
    queries_copy.wait_send()
    weight_copy.wait_send()
    swap.wait_send()
    gathered_copy.wait_send()
    terms_copy.wait_recv()
    own_copy.wait()
    terms_copy.wait_send()


def per_device(queries, k_cache, v_cache, o_weight, group_size, group_start, cache_len, owner):
    requests = group_size.shape[0]
    slots, width = k_cache.shape
    rows, columns = o_weight.shape
    chips = lax.axis_size("seq") // 2
    heads = lax.axis_size("head")
    hbm = pl.BlockSpec(memory_space=pl.ANY)
    vmem = pl.BlockSpec(memory_space=pltpu.VMEM)
    smem = pl.BlockSpec(memory_space=pltpu.SMEM)
    terms = pl.pallas_call(
        kernel,
        out_shape=jax.ShapeDtypeStruct((2 * heads, 8, columns), jnp.float32),
        in_specs=[hbm, hbm, hbm, hbm, hbm, hbm, hbm, hbm],
        out_specs=hbm,
        scratch_shapes=[
            pltpu.VMEM(queries.shape, jnp.bfloat16),
            pltpu.SMEM((requests,), jnp.int32),
            pltpu.SMEM((requests,), jnp.int32),
            pltpu.SMEM((requests,), jnp.int32),
            pltpu.SMEM((requests,), jnp.int32),
            pltpu.VMEM((2, slots, width // 2), jnp.bfloat16),
            pltpu.VMEM((2, width // 2, slots), jnp.bfloat16),
            pltpu.VMEM((2, slots, width // 2), jnp.bfloat16),
            pltpu.VMEM((2, rows // 2, columns), jnp.bfloat16),
            pltpu.VMEM((BLOCK, 16, HEAD_DIM), jnp.bfloat16),
            pltpu.VMEM((24, HEAD_DIM), jnp.float32),
            pltpu.VMEM((24, HEAD_DIM), jnp.float32),
            pltpu.VMEM((chips, 16, HEAD_DIM), jnp.float32),
            pltpu.VMEM((2, 8, columns), jnp.float32),
            pltpu.SemaphoreType.DMA((11,)),
            pltpu.SemaphoreType.DMA((5,)),
            pltpu.SemaphoreType.DMA((5,)),
            pltpu.SemaphoreType.REGULAR,
        ],
        compiler_params=pltpu.CompilerParams(
            collective_id=0, has_side_effects=True, vmem_limit_bytes=56 * 1024 * 1024
        ),
    )(queries, k_cache, v_cache, o_weight, group_size, group_start, cache_len, owner)
    return jnp.sum(terms, axis=0)[:requests].astype(jnp.bfloat16)


def solution(mesh):
    in_specs = (
        P("seq", "head"),
        P("seq", "head"),
        P("seq", "head"),
        P("head", "seq"),
        P(),
        P(),
        P(),
        P(),
    )
    out_specs = P(None, "seq")
    return jax.shard_map(
        per_device, mesh=mesh, in_specs=in_specs, out_specs=out_specs, check_vma=False
    )
```

```python
import functools

import jax
import jax.numpy as jnp
from jax import lax
from jax.experimental import pallas as pl
from jax.experimental.pallas import tpu as pltpu
from jax.sharding import PartitionSpec as P

HEAD_DIM = 128
MESH = pl.DeviceIdType.MESH
LOG2E = 1.4426950408889634
SCALE = HEAD_DIM ** (-0.5)
EXPO = SCALE * LOG2E
NEG = -1e30 / SCALE
BLOCK = 32
WIDTH = 4
PARTS = 4
CHUNK = 1024
TURN = 256


def attend(query, k_turned, v_vmem, live, slots):
    lane = lax.broadcasted_iota(jnp.int32, (8, CHUNK), 1)
    per_part = slots // PARTS

    def score_part(part):
        scores = []
        for first in range(part * per_part, (part + 1) * per_part, CHUNK):
            keys = k_turned[:, first : first + CHUNK]
            score = jnp.dot(query, keys, preferred_element_type=jnp.float32)
            scores.append(jnp.where(lane < live - first, score, NEG))
        return scores

    def value_part(part, scores):
        peak = functools.reduce(jnp.maximum, scores)
        peak = jnp.max(peak, axis=1, keepdims=True)
        total = jnp.zeros((8, CHUNK), jnp.float32)
        summed = jnp.zeros((8, HEAD_DIM), jnp.float32)
        for step, score in enumerate(scores):
            first = part * per_part + step * CHUNK
            expo = jnp.exp2((score - peak) * EXPO)
            total = total + expo
            summed = summed + jnp.dot(
                expo.astype(jnp.bfloat16),
                v_vmem[first : first + CHUNK, :],
                preferred_element_type=jnp.float32,
            )
        return peak, jnp.sum(total, axis=1, keepdims=True), summed

    found = []
    scores = score_part(0)
    for part in range(1, PARTS):
        following = score_part(part)
        found.append(value_part(part - 1, scores))
        scores = following
    found.append(value_part(PARTS - 1, scores))
    top = functools.reduce(jnp.maximum, [peak for peak, _, _ in found])
    total = jnp.zeros((8, 1), jnp.float32)
    summed = jnp.zeros((8, HEAD_DIM), jnp.float32)
    for peak, part_total, part_summed in found:
        shrink = jnp.exp2((peak - top) * EXPO)
        total = total + part_total * shrink
        summed = summed + part_summed * shrink
    shape = (8, HEAD_DIM)
    return jnp.broadcast_to(top, shape), jnp.broadcast_to(total, shape), summed


def far_first(length, width):
    steps = [(z, y) for z in range(length) for y in range(width)]
    steps.sort(key=lambda s: -(min(s[0], length - s[0]) + min(s[1], width - s[1])))
    return steps


def kernel(
    q_hbm,
    k_hbm,
    v_hbm,
    w_hbm,
    size_hbm,
    start_hbm,
    length_hbm,
    owner_hbm,
    terms,
    q_ref,
    size_ref,
    start_ref,
    length_ref,
    owner_ref,
    k_vmem,
    k_turned,
    v_vmem,
    w_vmem,
    q_all,
    swap_out,
    swap_in,
    gathered,
    product,
    load_sem,
    send_sem,
    recv_sem,
    late_sem,
):
    me = lax.axis_index("seq")
    x = lax.axis_index("head")
    slots = k_hbm.shape[0]
    requests = size_ref.shape[0]
    base = (me // BLOCK) * BLOCK
    off = me - base
    core = me % 2
    chip = me // 2
    other = me + 1 - 2 * core
    chips = lax.axis_size("seq") // 2
    heads = lax.axis_size("head")
    half = w_hbm.shape[0] // 2

    columns = [
        pl.ds(pl.multiple_of((1 - core) * HEAD_DIM, HEAD_DIM), HEAD_DIM),
        pl.ds(pl.multiple_of(core * HEAD_DIM, HEAD_DIM), HEAD_DIM),
    ]
    loads = []
    for hbm, vmem in ((k_hbm, k_vmem), (v_hbm, v_vmem)):
        for turn in range(2):
            loads.append(
                pltpu.make_async_copy(
                    hbm.at[:, columns[turn]], vmem.at[turn], load_sem.at[len(loads)]
                )
            )
    mine = pl.ds(pl.multiple_of(core * half, half), half)
    theirs = pl.ds(pl.multiple_of((1 - core) * half, half), half)
    loads.append(pltpu.make_async_copy(w_hbm.at[mine], w_vmem.at[0], load_sem.at[4]))
    facts_in = [pltpu.make_async_copy(a, b, load_sem.at[5 + i]) for i, (a, b) in enumerate(((size_hbm, size_ref), (start_hbm, start_ref), (length_hbm, length_ref), (owner_hbm, owner_ref)))]
    query_in = pltpu.make_async_copy(q_hbm, q_ref, load_sem.at[9])
    query_in.start()

    z, y = chip // WIDTH, chip % WIDTH
    quarter = BLOCK // (2 * WIDTH)
    z_first = (z // quarter) * quarter

    early = me < BLOCK

    z_own = z % quarter
    z_there = (z_own, z_own + 1 - 2 * (z_own % 2), (z_own + 2) % quarter, quarter - 1 - z_own)
    block_steps = [(way, dy) for way in range(quarter) for dy in range(WIDTH)]
    block_steps.sort(key=lambda s: -(s[0] + min(s[1], WIDTH - s[1])))

    def block_peers():
        for way, dy in block_steps:
            there = 2 * ((z_first + z_there[way]) * WIDTH + (y + dy) % WIDTH)
            yield there + 1 - core
            if (way, dy) != (0, 0):
                yield there + core

    def same_core_peers():
        for way, dy in block_steps:
            if (way, dy) != (0, 0):
                yield 2 * ((z_first + z_there[way]) * WIDTH + (y + dy) % WIDTH) + core

    other_half = ((me // BLOCK + 1) % 2) * quarter

    def other_half_peers():
        for dz, dy in far_first(quarter, WIDTH):
            yield 2 * ((other_half + (z + dz) % quarter) * WIDTH + (y + dy) % WIDTH) + core

    barrier = pltpu.get_barrier_semaphore()

    for peer in block_peers():
        pl.semaphore_signal(barrier, 1, device_id={"seq": peer}, device_id_type=MESH)
    for load in facts_in + loads:
        load.start()

    @pl.when(early)
    def _():
        for peer in other_half_peers():
            pl.semaphore_signal(barrier, 1, device_id={"seq": peer}, device_id_type=MESH)

    for step in range(1, heads):
        across = (x + step) % heads
        for seq in (me, other):
            pl.semaphore_signal(
                barrier, 1, device_id={"seq": seq, "head": across}, device_id_type=MESH
            )

    query_in.wait()
    query = q_ref[...].astype(jnp.float32)
    rows = [query[:, h * HEAD_DIM : (h + 1) * HEAD_DIM] for h in range(16)]
    q_all[off] = jnp.concatenate(rows, axis=0).astype(jnp.bfloat16)
    @pl.when(early)
    def _():
        pl.semaphore_wait(barrier, (BLOCK - 1) + 2 * (heads - 1))

    @pl.when(jnp.logical_not(early))
    def _():
        pl.semaphore_wait(barrier, (BLOCK - 1) + BLOCK // 2 + 2 * (heads - 1))


    for peer in block_peers():
        pltpu.make_async_remote_copy(
            src_ref=q_all.at[off],
            dst_ref=q_all.at[off],
            send_sem=send_sem.at[0],
            recv_sem=recv_sem.at[0],
            device_id={"seq": peer},
            device_id_type=MESH,
        ).start()

    weight_copy = pltpu.make_async_remote_copy(
        src_ref=w_hbm.at[theirs],
        dst_ref=w_vmem.at[1],
        send_sem=send_sem.at[1],
        recv_sem=recv_sem.at[1],
        device_id={"seq": other},
        device_id_type=MESH,
    )


    for load in facts_in:
        load.wait()
    my_start = jnp.int32(0)
    my_length = jnp.int32(0)
    my_owner = jnp.int32(0)
    for r in range(requests):
        inside = (me >= start_ref[r]) & (me < start_ref[r] + size_ref[r])
        my_start = my_start + jnp.where(inside, start_ref[r], 0)
        my_length = my_length + jnp.where(inside, length_ref[r], 0)
        my_owner = my_owner + jnp.where(inside, owner_ref[r], 0)
    live = my_length - (me - my_start) * slots

    @pl.when(jnp.logical_not(early))
    def _():
        for peer in other_half_peers():
            pl.semaphore_signal(late_sem, 1, device_id={"seq": peer}, device_id_type=MESH)

    for turn in range(2):
        loads[turn].wait()
        for first in range(0, slots, TURN):
            rows = slice(first, first + TURN)
            k_turned[turn, :, rows] = k_vmem[turn, rows, :].T
    for load in loads[2:]:
        load.wait()
    weight_copy.start()
    queries_in = q_all.at[pl.ds(0, BLOCK - 1)]
    queries_copy = pltpu.make_async_remote_copy(
        src_ref=queries_in,
        dst_ref=queries_in,
        send_sem=send_sem.at[0],
        recv_sem=recv_sem.at[0],
        device_id={"seq": other},
        device_id_type=MESH,
    )
    queries_copy.wait_recv()
    query = q_all[lax.rem(my_owner, BLOCK)]
    first = core == 0

    theirs = attend(
        jnp.where(first, query[8:], query[:8]), k_turned.at[0], v_vmem.at[0], live, slots
    )
    for i in range(3):
        swap_out[8 * i : 8 * i + 8, :] = theirs[i]
    swap = pltpu.make_async_remote_copy(
        src_ref=swap_out,
        dst_ref=swap_in,
        send_sem=send_sem.at[2],
        recv_sem=recv_sem.at[2],
        device_id={"seq": other},
        device_id_type=MESH,
    )
    swap.start()
    top, total, summed = attend(
        jnp.where(first, query[:8], query[8:]), k_turned.at[1], v_vmem.at[1], live, slots
    )
    swap.wait_recv()
    their_top = swap_in[0:8, :]
    new_top = jnp.maximum(top, their_top)
    shrink = jnp.exp2((top - new_top) * EXPO)
    their_shrink = jnp.exp2((their_top - new_top) * EXPO)
    gathered[chip, 0:8, :] = summed * shrink + swap_in[16:24, :] * their_shrink
    total = total * shrink + swap_in[8:16, :] * their_shrink
    lane = lax.broadcasted_iota(jnp.int32, (8, HEAD_DIM), 1)
    row = lax.broadcasted_iota(jnp.int32, (8, HEAD_DIM), 0)
    facts = jnp.where(lane == row, new_top, 0.0) + jnp.where(lane == row + 8, total, 0.0)
    gathered[chip, 8:9, :] = jnp.sum(facts, axis=0, keepdims=True)

    def send_gathered(peer):
        pltpu.make_async_remote_copy(
            src_ref=gathered.at[chip, pl.ds(0, 9)],
            dst_ref=gathered.at[chip, pl.ds(0, 9)],
            send_sem=send_sem.at[3],
            recv_sem=recv_sem.at[3],
            device_id={"seq": peer},
            device_id_type=MESH,
        ).start()

    @pl.when(early)
    def _():
        for peer in same_core_peers():
            send_gathered(peer)
        pl.semaphore_wait(late_sem, BLOCK // 2)
        for peer in other_half_peers():
            send_gathered(peer)

    @pl.when(jnp.logical_not(early))
    def _():
        for there in (0, 1, 3, 2, 4, 8, 5, 7, 6, 9, 11, 10, 12, 13, 15, 14):
            send_gathered(2 * there + core)
        for peer in same_core_peers():
            send_gathered(peer)

    starts = jnp.zeros((8, chips), jnp.int32)
    ends = jnp.zeros((8, chips), jnp.int32)
    request = lax.broadcasted_iota(jnp.int32, (8, chips), 0)
    seq_of = 2 * lax.broadcasted_iota(jnp.int32, (8, chips), 1)
    for r in range(requests):
        starts = jnp.where(request == r, start_ref[r], starts)
        ends = jnp.where(request == r, start_ref[r] + size_ref[r], ends)
    member = ((seq_of >= starts) & (seq_of < ends)).astype(jnp.float32).astype(jnp.bfloat16)
    seq_down = 2 * lax.broadcasted_iota(jnp.int32, (chips, HEAD_DIM), 0)
    serves = [
        (seq_down >= start_ref[r]) & (seq_down < start_ref[r] + size_ref[r])
        for r in range(requests)
    ]

    gathered_in = gathered.at[pl.ds(0, chips - 1), pl.ds(0, 9)]
    gathered_copy = pltpu.make_async_remote_copy(
        src_ref=gathered_in,
        dst_ref=gathered_in,
        send_sem=send_sem.at[3],
        recv_sem=recv_sem.at[3],
        device_id={"seq": other},
        device_id_type=MESH,
    )
    gathered_copy.wait_recv()

    facts = gathered[:, 8, :]
    totals = pltpu.roll(facts, HEAD_DIM - 8, 1)
    tops = jnp.zeros((chips, HEAD_DIM), jnp.float32)
    for r in range(requests):
        top = jnp.max(jnp.where(serves[r], facts, NEG), axis=0, keepdims=True)
        tops = jnp.where(serves[r], top, tops)
    lane = lax.broadcasted_iota(jnp.int32, (chips, HEAD_DIM), 1)
    factor = jnp.exp2(jnp.where(lane < 8, (facts - tops) * EXPO, 0.0))
    scaled = factor * totals
    sums = jnp.ones((chips, HEAD_DIM), jnp.float32)
    for r in range(requests):
        total = jnp.sum(jnp.where(serves[r], scaled, 0.0), axis=0, keepdims=True)
        sums = jnp.where(serves[r], total, sums)
    factor = factor / sums
    pieces = [gathered[:, h, :] * factor[:, h : h + 1] for h in range(8)]
    weighted = jnp.concatenate(pieces, axis=1).astype(jnp.bfloat16)
    attended = jnp.dot(member, weighted, preferred_element_type=jnp.float32).astype(jnp.bfloat16)

    weight_copy.wait_recv()
    slot = 2 * x + core

    def final(which, seq, across):
        return pltpu.make_async_remote_copy(
            src_ref=product.at[which],
            dst_ref=terms.at[slot],
            send_sem=send_sem.at[4],
            recv_sem=recv_sem.at[4],
            device_id={"seq": seq, "head": across},
            device_id_type=MESH,
        )

    own_copy = pltpu.make_async_copy(product.at[core], terms.at[slot], load_sem.at[10])
    for to_core in (1, 0):
        which = (core + to_core) % 2
        product[to_core] = jnp.dot(
            attended, w_vmem[which], preferred_element_type=jnp.float32
        )
        for across in range(heads):

            @pl.when(jnp.logical_or(across != x, to_core != core))
            def _():
                final(to_core, me - core + to_core, across).start()

    own_copy.start()

    terms_in = terms.at[pl.ds(0, 2 * heads - 1)]
    terms_copy = pltpu.make_async_remote_copy(
        src_ref=terms_in,
        dst_ref=terms_in,
        send_sem=send_sem.at[4],
        recv_sem=recv_sem.at[4],
        device_id={"seq": other},
        device_id_type=MESH,
    )
    queries_copy.wait_send()
    weight_copy.wait_send()
    swap.wait_send()
    gathered_copy.wait_send()
    terms_copy.wait_recv()
    own_copy.wait()
    terms_copy.wait_send()


def per_device(queries, k_cache, v_cache, o_weight, group_size, group_start, cache_len, owner):
    requests = group_size.shape[0]
    slots, width = k_cache.shape
    rows, columns = o_weight.shape
    chips = lax.axis_size("seq") // 2
    heads = lax.axis_size("head")
    hbm = pl.BlockSpec(memory_space=pl.ANY)
    vmem = pl.BlockSpec(memory_space=pltpu.VMEM)
    smem = pl.BlockSpec(memory_space=pltpu.SMEM)
    terms = pl.pallas_call(
        kernel,
        out_shape=jax.ShapeDtypeStruct((2 * heads, 8, columns), jnp.float32),
        in_specs=[hbm, hbm, hbm, hbm, hbm, hbm, hbm, hbm],
        out_specs=hbm,
        scratch_shapes=[
            pltpu.VMEM(queries.shape, jnp.bfloat16),
            pltpu.SMEM((requests,), jnp.int32),
            pltpu.SMEM((requests,), jnp.int32),
            pltpu.SMEM((requests,), jnp.int32),
            pltpu.SMEM((requests,), jnp.int32),
            pltpu.VMEM((2, slots, width // 2), jnp.bfloat16),
            pltpu.VMEM((2, width // 2, slots), jnp.bfloat16),
            pltpu.VMEM((2, slots, width // 2), jnp.bfloat16),
            pltpu.VMEM((2, rows // 2, columns), jnp.bfloat16),
            pltpu.VMEM((BLOCK, 16, HEAD_DIM), jnp.bfloat16),
            pltpu.VMEM((24, HEAD_DIM), jnp.float32),
            pltpu.VMEM((24, HEAD_DIM), jnp.float32),
            pltpu.VMEM((chips, 16, HEAD_DIM), jnp.float32),
            pltpu.VMEM((2, 8, columns), jnp.float32),
            pltpu.SemaphoreType.DMA((11,)),
            pltpu.SemaphoreType.DMA((5,)),
            pltpu.SemaphoreType.DMA((5,)),
            pltpu.SemaphoreType.REGULAR,
        ],
        compiler_params=pltpu.CompilerParams(
            collective_id=0, has_side_effects=True, vmem_limit_bytes=56 * 1024 * 1024
        ),
    )(queries, k_cache, v_cache, o_weight, group_size, group_start, cache_len, owner)
    return jnp.sum(terms, axis=0)[:requests].astype(jnp.bfloat16)


def solution(mesh):
    in_specs = (
        P("seq", "head"),
        P("seq", "head"),
        P("seq", "head"),
        P("head", "seq"),
        P(),
        P(),
        P(),
        P(),
    )
    out_specs = P(None, "seq")
    return jax.shard_map(
        per_device, mesh=mesh, in_specs=in_specs, out_specs=out_specs, check_vma=False
    )
```
